32 devices in a mesh: grp: 2 (over x), dp: 8 (over z, y), layer: 2 (over core).
Axes of the slice: x: 2, y: 2, z: 4, core: 2. Of those that a mesh axis runs over, the one named last changes fastest.
Arguments:
- train_inputs: bfloat16 [128, 4, 32, 4096], P(('grp', 'dp'), 'layer'), parts along dimension 0, may hold values from -6 to 6
- train_grads: bfloat16 [128, 4, 32, 4096], P(('grp', 'dp'), 'layer'), parts along dimension 0, may hold values from -6 to 6
- train_ids: int32 [128, 32], P(('grp', 'dp')), parts along dimension 0, may hold values from 0 to 128001, as said below
- weight_codes: int32 [128, 32], P(('grp', 'dp')), parts along dimension 0, may hold values from 0 to 15
- code_table: float32 [16], replicated, may hold values from -2 to 2
- assignment: int32 [4], replicated, may hold values from 0 to 3, each once
- basis_in: bfloat16 [4, 64, 4096], replicated, may hold values from -0.09375 to 0.09375
- basis_out: bfloat16 [4, 64, 4096], replicated, may hold values from -0.09375 to 0.09375
- query_proj: bfloat16 [256, 16384], P(('grp', 'dp'), 'layer'), parts along dimension 0, may hold values from -0.0078125 to 0.0078125
Outputs:
- scores: float32 [128, 128], P(('dp', 'layer'), 'grp'), parts along dimension 1
- score_tangent: float32 [128, 128], P(('dp', 'layer'), 'grp'), parts along dimension 1
The draws below stay inside these ranges and needn't reach their ends.
There are 2 independent parts, one for each index of `grp`. The reference program is written for one: setup_inputs(seed, part) draws one part's arguments, and reference() takes and returns one part's arrays. A program takes and returns all parts, laid end to end along the dimension named above; an argument that names none is the same for every part. Nothing has to cross between parts.
Inputs may be any that keep to these rules, and one draw needn't show every extreme that they name: `train_ids`: each training example's real tokens come first, at least 8 of them, followed by one or more padding positions holding 128001.
All inputs are finite; a program needn't handle non-finite values.
Results may differ from the reference program's by a relative error of at most 0.005.
Values may be sent and summed in bfloat16 or wider, within the bound.
A program may use at most 128 MiB of HBM per device.

```python
import jax
import jax.numpy as jnp
from jax import lax

D = 4096
RANK = 64
TOK = 32
NCODES = 16
LAYERS = 4
EXAMPLES = 64
QUERIES = 128


def draw_train_ids(key, part):
    key = jax.random.fold_in(key, 11)
    key_len, key_ids = jax.random.split(key)
    lengths = jax.random.randint(key_len, (EXAMPLES, 1), TOK // 4, TOK)
    tokens = jax.random.randint(key_ids, (EXAMPLES, TOK), 0, 128000)
    tokens = tokens.at[0, 0].set(0)
    position = jnp.arange(TOK)[None, :]
    return jnp.where(position < lengths, tokens, 128001).astype(jnp.int32)


def with_ends(result, key, low, largest):
    longest = result.shape.index(max(result.shape))
    spots = []
    for shift in (0, 1):
        where = [jax.random.randint(jax.random.fold_in(key, axis), (), 0, length) for axis, length in enumerate(result.shape)]
        where[longest] = (where[longest] + shift) % result.shape[longest]
        spots.append(tuple(where))
    return result.at[spots[0]].set(low).at[spots[1]].set(largest)


def levels(stream_key, shape, pieces, low, top_value):
    factor_of = 1.0
    for dim, parts in pieces:
        heights = jax.random.uniform(jax.random.fold_in(jax.random.fold_in(stream_key, 6), dim), (parts,), jnp.float32, low / len(pieces), top_value / len(pieces))
        factor_of = factor_of * jnp.repeat(jnp.exp(heights), shape[dim] // parts).reshape((-1,) + (1,) * (len(shape) - 1 - dim))
    return factor_of


def centred(rng, extent, deviation, limit, pieces=(), kind=jnp.bfloat16):
    level = levels(rng, extent, pieces, -0.22, 0.18) if pieces else 1.0
    array = jax.random.normal(rng, extent, jnp.float32) * deviation * level
    return jnp.minimum(jnp.maximum(array, -limit), limit).astype(kind)


def setup_inputs(seed: int = 0, part: int = 0) -> dict:
    keys = jax.random.split(jax.random.key(seed), 10)
    part_splits = jax.random.split(jax.random.fold_in(keys[9], part), 10)
    return {
        "train_inputs": centred(part_splits[0], (EXAMPLES, LAYERS, TOK, D), 1.0, 6.0, ((0, 8), (1, 2))),
        "train_grads": centred(part_splits[1], (EXAMPLES, LAYERS, TOK, D), 1.0, 6.0, ((0, 8), (1, 2))),
        "train_ids": draw_train_ids(jax.random.fold_in(jax.random.fold_in(keys[9], part), 71), part),
        "weight_codes": with_ends(jax.random.randint(part_splits[3], (EXAMPLES, TOK), 0, NCODES), jax.random.fold_in(part_splits[3], 1), 0, NCODES - 1).astype(jnp.int32),
        "code_table": jnp.clip(jax.random.uniform(keys[4], (NCODES,), jnp.float32, -2.0, 2.0), -2.0, 2.0),
        "assignment": jax.random.permutation(keys[5], LAYERS).astype(jnp.int32),
        "basis_in": centred(keys[6], (LAYERS, RANK, D), D ** -0.5, 0.09375),
        "basis_out": centred(keys[7], (LAYERS, RANK, D), D ** -0.5, 0.09375),
        "query_proj": centred(part_splits[8], (QUERIES, LAYERS * RANK * RANK), (TOK * LAYERS * RANK * RANK) ** -0.5, 0.0078125, ((0, 8), (1, 2))),
    }


pad_token = 128001


def reference(train_inputs, train_grads, train_ids, weight_codes, code_table, assignment, basis_in, basis_out, query_proj):
    keep = (train_ids != pad_token).astype(jnp.float32).reshape(-1)
    direction = code_table[weight_codes].reshape(-1)
    plain = []
    tangent = []
    for slot in range(LAYERS):
        layer_id = assignment[slot]
        p_in = lax.dynamic_index_in_dim(basis_in, layer_id, 0, keepdims=False)
        p_out = lax.dynamic_index_in_dim(basis_out, layer_id, 0, keepdims=False)
        rows_x = train_inputs[:, slot].reshape(EXAMPLES * TOK, D)
        rows_g = train_grads[:, slot].reshape(EXAMPLES * TOK, D)
        in_proj = jnp.dot(p_in, rows_x.T, preferred_element_type=jnp.float32).astype(jnp.bfloat16)
        out_proj = jnp.dot(p_out, rows_g.T, preferred_element_type=jnp.float32)
        kept = (out_proj * keep).astype(jnp.bfloat16)
        weighted = (out_proj * keep * direction).astype(jnp.bfloat16)
        in_three = in_proj.reshape(RANK, EXAMPLES, TOK).astype(jnp.float32)
        kept_three = kept.reshape(RANK, EXAMPLES, TOK).astype(jnp.float32)
        weighted_three = weighted.reshape(RANK, EXAMPLES, TOK).astype(jnp.float32)
        grad_proj = jnp.einsum('aet,bet->eab', kept_three, in_three).astype(jnp.bfloat16)
        grad_tan = jnp.einsum('aet,bet->eab', weighted_three, in_three).astype(jnp.bfloat16)
        plain.append(grad_proj.reshape(EXAMPLES, RANK * RANK))
        tangent.append(grad_tan.reshape(EXAMPLES, RANK * RANK))
    grad_all = jnp.concatenate(plain, axis=1)
    tan_all = jnp.concatenate(tangent, axis=1)
    scores = jnp.dot(query_proj, grad_all.T, preferred_element_type=jnp.float32)
    score_tangent = jnp.dot(query_proj, tan_all.T, preferred_element_type=jnp.float32)
    return scores, score_tangent
```

```python
import functools

import jax
import jax.numpy as jnp
from jax import lax
from jax.experimental import pallas as pl
from jax.experimental.pallas import tpu as pltpu
from jax.sharding import PartitionSpec as P

pad_token = 128001
MESH = pl.DeviceIdType.MESH
NT = (((1,), (1,)), ((), ()))


def loop(count, body):
    if count <= 4:
        for step in range(count):
            body(step)
    else:
        lax.fori_loop(0, count, lambda step, carry: (body(step), carry)[1], 0)


def kernel(
    blocks, x_hbm, g_hbm, ids_ref, codes_ref, table_ref, assign_ref, bin_hbm, bout_hbm, q_hbm,
    out_ref,
    x_buf, g_buf, bin_buf, bout_buf, q_buf, in_own, kept_own, in_all, kept_all, kept_wide, grads, part, sums,
    load_sem, basis_sem, q_send, q_recv, relay_send, in_send, kept_send, in_recv, kept_recv, sum_send, sum_recv,
):
    examples, slots, tokens, width = x_hbm.shape
    chips, rank = bin_hbm.shape[:2]
    lanes = examples * tokens
    features = rank * rank
    cores = chips // slots
    kinds = 2 * examples
    share = q_hbm.shape[0] // cores
    grp_dp = lax.axis_index("dp")
    core = lax.axis_index("layer")
    block = grp_dp // chips
    chip = lax.rem(grp_dp, chips)
    base = block * chips

    load_bin = pltpu.make_async_copy(bin_hbm, bin_buf, basis_sem.at[0])
    load_bout = pltpu.make_async_copy(bout_hbm, bout_buf, basis_sem.at[1])
    loads_x = [pltpu.make_async_copy(x_hbm.at[:, k], x_buf.at[k], load_sem.at[k, 0]) for k in range(slots)]
    loads_g = [pltpu.make_async_copy(g_hbm.at[:, k], g_buf.at[k], load_sem.at[k, 1]) for k in range(slots)]
    load_bin.start()
    loads_x[0].start()
    load_bout.start()
    loads_g[0].start()
    for k in range(1, slots):
        loads_x[k].start()
        loads_g[k].start()

    barrier = pltpu.get_barrier_semaphore()
    for other in range(1, chips * cores):
        place = lax.rem(chip * cores + core + other, chips * cores)
        pl.semaphore_signal(
            barrier, inc=1, device_id={"dp": base + place // cores, "layer": lax.rem(place, cores)}, device_id_type=MESH
        )

    def greet(step):
        far = lax.rem(block + step + 1, blocks) * chips
        for k in range(slots):
            pl.semaphore_signal(
                barrier, inc=1, device_id={"dp": far + k * cores + core, "layer": chip // slots}, device_id_type=MESH
            )

    loop(blocks - 1, greet)
    pl.semaphore_wait(barrier, chips * cores - 1 + slots * (blocks - 1))

    to_core = lax.rem(chip, cores)
    slot_of = [core * slots + k for k in range(slots)]
    stays = [jnp.logical_and(chip == slot_of[k], to_core == core) for k in range(slots)]

    def q_copy(k):
        return pltpu.make_async_remote_copy(
            src_ref=q_hbm.at[:, pl.ds(k * features, features)],
            dst_ref=q_buf.at[chip],
            send_sem=q_send.at[k],
            recv_sem=q_recv.at[chip],
            device_id={"dp": base + slot_of[k], "layer": to_core},
            device_id_type=MESH,
        )

    for k in range(slots):

        @pl.when(jnp.logical_not(stays[k]))
        def _():
            q_copy(k).start()

        @pl.when(stays[k])
        def _():
            pltpu.make_async_copy(
                q_hbm.at[:, pl.ds(k * features, features)], q_buf.at[chip], q_recv.at[chip]
            ).start()

    ids = ids_ref[...]
    codes = codes_ref[...]
    keep8 = (ids != pad_token).astype(jnp.float32)
    dir8 = jnp.zeros(codes.shape, jnp.float32)
    for code in range(table_ref.shape[0]):
        dir8 = jnp.where(codes == code, table_ref[code], dir8)
    keep = jnp.concatenate([keep8[e : e + 1] for e in range(examples)], axis=1)
    direction = jnp.concatenate([dir8[e : e + 1] for e in range(examples)], axis=1)
    dir_high = direction.astype(jnp.bfloat16).astype(jnp.float32)
    dir_low = direction - dir_high
    row16 = lax.broadcasted_iota(jnp.int32, (16, lanes), 0)
    dir_rows = jnp.where(row16 == 0, dir_high, jnp.where(row16 == 1, dir_low, 0.0)).astype(jnp.bfloat16)

    mine = block * slots + chip // cores

    def factor_copy(k, far_block, own, every, send, recv):
        return pltpu.make_async_remote_copy(
            src_ref=own.at[k],
            dst_ref=every.at[mine],
            send_sem=send.at[k, far_block],
            recv_sem=recv.at[mine],
            device_id={"dp": far_block * chips + slot_of[k], "layer": to_core},
            device_id_type=MESH,
        )

    def send_factor(k, own, every, send, recv):
        def far(step):
            factor_copy(k, lax.rem(block + step + 1, blocks), own, every, send, recv).start()

        loop(blocks - 1, far)

        @pl.when(jnp.logical_not(stays[k]))
        def _():
            factor_copy(k, block, own, every, send, recv).start()

        @pl.when(stays[k])
        def _():
            pltpu.make_async_copy(own.at[k], every.at[mine], recv.at[mine]).start()

    def sent_factor(k, own, every, send, recv):
        def far(step):
            factor_copy(k, lax.rem(block + step + 1, blocks), own, every, send, recv).wait_send()

        loop(blocks - 1, far)

        @pl.when(jnp.logical_not(stays[k]))
        def _():
            factor_copy(k, block, own, every, send, recv).wait_send()

    def relay(h):
        source = h * cores + core
        return pltpu.make_async_remote_copy(
            src_ref=q_buf.at[source],
            dst_ref=q_buf.at[source],
            send_sem=relay_send.at[h],
            recv_sem=q_recv.at[source],
            device_id={"layer": 1 - core},
            device_id_type=MESH,
        )

    in_args = (in_own, in_all, in_send, in_recv)
    kept_args = (kept_own, kept_all, kept_send, kept_recv)
    for k in range(slots):
        layer_id = assign_ref[core * slots + k]
        if k == 0:
            load_bin.wait()
        loads_x[k].wait()
        in_proj = lax.dot_general(
            bin_buf[layer_id], x_buf[k].reshape(lanes, width), NT, preferred_element_type=jnp.float32
        )
        in_own[k] = in_proj.astype(jnp.bfloat16)
        send_factor(k, *in_args)
        if k == 0:
            load_bout.wait()
        loads_g[k].wait()
        out_proj = lax.dot_general(
            bout_buf[layer_id], g_buf[k].reshape(lanes, width), NT, preferred_element_type=jnp.float32
        )
        kept_own[k, :rank] = (out_proj * keep).astype(jnp.bfloat16)
        kept_own[k, rank:] = dir_rows
        send_factor(k, *kept_args)

    for h in range(chips // cores):
        relay(h).wait_recv()
        relay(h).start()

    row = lax.broadcasted_iota(jnp.int32, (kinds, lanes), 0)
    lane = lax.broadcasted_iota(jnp.int32, (kinds, lanes), 1)
    own_tokens = lane // tokens == lax.rem(row, examples)
    group = 256 // rank

    def product(step):
        near = lax.rem(block + step // (chips // cores), blocks)
        at = near * (chips // cores) + lax.rem(step, chips // cores)
        pltpu.make_async_copy(in_all.at[at], in_all.at[at], in_recv.at[at]).wait()
        pltpu.make_async_copy(kept_all.at[at], kept_all.at[at], kept_recv.at[at]).wait()
        in_block = in_all[at]
        kept_wide[...] = kept_all[at].astype(jnp.float32)
        dirs = kept_wide[rank : rank + 1] + kept_wide[rank + 1 : rank + 2]
        scale = jnp.where(own_tokens, jnp.where(row < examples, 1.0, dirs), 0.0)
        total = None
        for i in range(group):
            left = jnp.concatenate(
                [
                    (kept_wide[a : a + 1] * scale).astype(jnp.bfloat16)
                    for a in range(i, rank, group)
                ],
                axis=0,
            )
            pieces = [jnp.zeros_like(in_block)] * group
            pieces[i] = in_block
            right = jnp.concatenate(pieces, axis=0)
            term = lax.dot_general(left, right, NT, preferred_element_type=jnp.float32)
            total = term if total is None else total + term
        rounded = total.astype(jnp.bfloat16)
        flat = jnp.concatenate(
            [rounded[a * kinds : (a + 1) * kinds] for a in range(rank // group)], axis=1
        )
        grads[pl.ds(pl.multiple_of(at * kinds, kinds), kinds)] = flat

    count = blocks * (chips // cores)
    loop(count, product)

    for h in range(chips // cores):
        source = h * cores + 1 - core
        pltpu.make_async_copy(q_buf.at[source], q_buf.at[source], q_recv.at[source]).wait()
    scores = lax.dot_general(
        q_buf[...].reshape(chips * q_buf.shape[1], features), grads[...], NT, preferred_element_type=jnp.float32
    )
    for place in range(chips * cores):
        part[place] = scores[place * share : (place + 1) * share]

    here = chip * cores + core

    def sum_copy(other):
        place = lax.rem(here + other, chips * cores)
        return pltpu.make_async_remote_copy(
            src_ref=part.at[place],
            dst_ref=sums.at[here],
            send_sem=sum_send.at[other],
            recv_sem=sum_recv.at[here],
            device_id={"dp": base + place // cores, "layer": lax.rem(place, cores)},
            device_id_type=MESH,
        )

    for other in range(1, chips * cores):
        sum_copy(other).start()
    pltpu.make_async_copy(part.at[here], sums.at[here], sum_recv.at[here]).start()
    for place in range(chips * cores):
        pltpu.make_async_copy(sums.at[place], sums.at[place], sum_recv.at[place]).wait()
    for c in range(cores):
        total = sums[c]
        for j in range(1, chips):
            total = total + sums[j * cores + c]
        out_ref[c] = total

    for k in range(slots):

        @pl.when(jnp.logical_not(stays[k]))
        def _():
            q_copy(k).wait_send()

        sent_factor(k, *in_args)
        sent_factor(k, *kept_args)
    for h in range(chips // cores):
        relay(h).wait_send()
    for other in range(1, chips * cores):
        sum_copy(other).wait_send()


def per_device(blocks, x, g, ids, codes, table, assignment, basis_in, basis_out, query):
    examples, slots, tokens, width = x.shape
    chips, rank = basis_in.shape[:2]
    cores = chips // slots
    lanes = examples * tokens
    features = rank * rank
    count = blocks * (chips // cores)
    kinds = 2 * examples
    queries = query.shape[0]
    share = queries // cores
    any_spec = pl.BlockSpec(memory_space=pl.ANY)
    vmem = pl.BlockSpec(memory_space=pltpu.VMEM)
    smem = pl.BlockSpec(memory_space=pltpu.SMEM)
    bf16, f32 = jnp.bfloat16, jnp.float32
    dma = pltpu.SemaphoreType.DMA
    summed = pl.pallas_call(
        functools.partial(kernel, blocks),
        out_shape=jax.ShapeDtypeStruct((cores, share, count * kinds), f32),
        in_specs=[any_spec, any_spec, vmem, vmem, smem, smem, any_spec, any_spec, any_spec],
        out_specs=vmem,
        scratch_shapes=[
            pltpu.VMEM((slots, examples, tokens, width), bf16),
            pltpu.VMEM((slots, examples, tokens, width), bf16),
            pltpu.VMEM(basis_in.shape, bf16),
            pltpu.VMEM(basis_out.shape, bf16),
            pltpu.VMEM((chips, queries, features), bf16),
            pltpu.VMEM((slots, rank, lanes), bf16),
            pltpu.VMEM((slots, rank + 16, lanes), bf16),
            pltpu.VMEM((count, rank, lanes), bf16),
            pltpu.VMEM((count, rank + 16, lanes), bf16),
            pltpu.VMEM((rank + 16, lanes), f32),
            pltpu.VMEM((count * kinds, features), bf16),
            pltpu.VMEM((chips * cores, share, count * kinds), f32),
            pltpu.VMEM((chips * cores, share, count * kinds), f32),
            dma((slots, 2)),
            dma((2,)),
            dma((slots,)),
            dma((chips,)),
            dma((chips // cores,)),
            dma((slots, blocks)),
            dma((slots, blocks)),
            dma((count,)),
            dma((count,)),
            dma((chips * cores,)),
            dma((chips * cores,)),
        ],
        compiler_params=pltpu.CompilerParams(
            collective_id=0, has_side_effects=True, vmem_limit_bytes=48 * 1024 * 1024
        ),
    )(x, g, ids, codes, table, assignment, basis_in, basis_out, query)
    split = summed.reshape(cores, share, count, 2, examples).transpose(3, 1, 2, 0, 4)
    split = split.reshape(2, share, count * cores * examples)
    return split[0], split[1]


def solution(mesh):
    placed = (
        P(("grp", "dp"), "layer", None, None),
        P(("grp", "dp"), "layer", None, None),
        P(("grp", "dp"), None),
        P(("grp", "dp"), None),
        P(),
        P(),
        P(),
        P(),
        P(("grp", "dp"), "layer"),
    )

    def run(*args):
        chips = args[5].shape[0]
        return jax.shard_map(
            functools.partial(per_device, mesh.shape["dp"] // chips),
            mesh=mesh,
            in_specs=placed,
            out_specs=(P(("dp", "layer"), "grp"), P(("dp", "layer"), "grp")),
            check_vma=False,
        )(*args)

    return run
```

```python
import functools

import jax
import jax.numpy as jnp
from jax import lax
from jax.experimental import pallas as pl
from jax.experimental.pallas import tpu as pltpu
from jax.sharding import PartitionSpec as P

pad_token = 128001
MESH = pl.DeviceIdType.MESH
NT = (((1,), (1,)), ((), ()))


def loop(count, body):
    if count <= 4:
        for step in range(count):
            body(step)
    else:
        lax.fori_loop(0, count, lambda step, carry: (body(step), carry)[1], 0)


def kernel(
    blocks, x_hbm, g_hbm, ids_hbm, codes_hbm, table_hbm, assign_hbm, bin_hbm, bout_hbm, q_hbm,
    scores_hbm, tangent_hbm,
    x_buf, g_buf, bin_buf, bout_buf, q_buf, in_own, kept_own, in_all, kept_all, kept_wide, grads, part, sums,
    ids_ref, codes_ref, table_ref, assign_ref, result,
    load_sem, basis_sem, q_send, q_recv, relay_send, in_send, kept_send, in_recv, kept_recv, sum_send, sum_recv, small_sem, result_sem,
):
    examples, slots, tokens, width = x_hbm.shape
    chips, rank = bin_hbm.shape[:2]
    lanes = examples * tokens
    features = rank * rank
    cores = chips // slots
    kinds = 2 * examples
    share = q_hbm.shape[0] // cores
    grp_dp = lax.axis_index("dp")
    core = lax.axis_index("layer")
    block = grp_dp // chips
    chip = lax.rem(grp_dp, chips)
    base = block * chips

    load_bin = pltpu.make_async_copy(bin_hbm, bin_buf, basis_sem.at[0])
    load_bout = pltpu.make_async_copy(bout_hbm, bout_buf, basis_sem.at[1])
    loads_x = [pltpu.make_async_copy(x_hbm.at[:, k], x_buf.at[k], load_sem.at[k, 0]) for k in range(slots)]
    loads_g = [pltpu.make_async_copy(g_hbm.at[:, k], g_buf.at[k], load_sem.at[k, 1]) for k in range(slots)]
    smalls = [
        pltpu.make_async_copy(source, target, small_sem.at[at])
        for at, (source, target) in enumerate(
            ((assign_hbm, assign_ref), (table_hbm, table_ref), (ids_hbm, ids_ref), (codes_hbm, codes_ref))
        )
    ]
    for small in smalls:
        small.start()
    load_bin.start()
    loads_x[0].start()
    load_bout.start()
    loads_g[0].start()
    for k in range(1, slots):
        loads_x[k].start()
        loads_g[k].start()

    barrier = pltpu.get_barrier_semaphore()
    for other in range(1, chips * cores):
        place = lax.rem(chip * cores + core + other, chips * cores)
        pl.semaphore_signal(
            barrier, inc=1, device_id={"dp": base + place // cores, "layer": lax.rem(place, cores)}, device_id_type=MESH
        )

    def greet(step):
        far = lax.rem(block + step + 1, blocks) * chips
        for k in range(slots):
            pl.semaphore_signal(
                barrier, inc=1, device_id={"dp": far + k * cores + core, "layer": chip // slots}, device_id_type=MESH
            )

    loop(blocks - 1, greet)
    pl.semaphore_wait(barrier, chips * cores - 1 + slots * (blocks - 1))

    to_core = lax.rem(chip, cores)
    slot_of = [core * slots + k for k in range(slots)]
    stays = [jnp.logical_and(chip == slot_of[k], to_core == core) for k in range(slots)]

    def q_copy(k):
        return pltpu.make_async_remote_copy(
            src_ref=q_hbm.at[:, pl.ds(k * features, features)],
            dst_ref=q_buf.at[chip],
            send_sem=q_send.at[k],
            recv_sem=q_recv.at[chip],
            device_id={"dp": base + slot_of[k], "layer": to_core},
            device_id_type=MESH,
        )

    for k in range(slots):

        @pl.when(jnp.logical_not(stays[k]))
        def _():
            q_copy(k).start()

        @pl.when(stays[k])
        def _():
            pltpu.make_async_copy(
                q_hbm.at[:, pl.ds(k * features, features)], q_buf.at[chip], q_recv.at[chip]
            ).start()

    for small in smalls:
        small.wait()
    ids = ids_ref[...]
    codes = codes_ref[...]
    keep8 = (ids != pad_token).astype(jnp.float32)
    dir8 = jnp.zeros(codes.shape, jnp.float32)
    for code in range(table_ref.shape[0]):
        dir8 = jnp.where(codes == code, table_ref[code], dir8)
    keep = jnp.concatenate([keep8[e : e + 1] for e in range(examples)], axis=1)
    direction = jnp.concatenate([dir8[e : e + 1] for e in range(examples)], axis=1)
    dir_high = direction.astype(jnp.bfloat16).astype(jnp.float32)
    dir_low = direction - dir_high
    row16 = lax.broadcasted_iota(jnp.int32, (16, lanes), 0)
    dir_rows = jnp.where(row16 == 0, dir_high, jnp.where(row16 == 1, dir_low, 0.0)).astype(jnp.bfloat16)

    mine = block * slots + chip // cores

    def factor_copy(k, far_block, own, every, send, recv):
        return pltpu.make_async_remote_copy(
            src_ref=own.at[k],
            dst_ref=every.at[mine],
            send_sem=send.at[k, far_block],
            recv_sem=recv.at[mine],
            device_id={"dp": far_block * chips + slot_of[k], "layer": to_core},
            device_id_type=MESH,
        )

    def send_factor(k, own, every, send, recv):
        def far(step):
            factor_copy(k, lax.rem(block + step + 1, blocks), own, every, send, recv).start()

        loop(blocks - 1, far)

        @pl.when(jnp.logical_not(stays[k]))
        def _():
            factor_copy(k, block, own, every, send, recv).start()

        @pl.when(stays[k])
        def _():
            pltpu.make_async_copy(own.at[k], every.at[mine], recv.at[mine]).start()

    def sent_factor(k, own, every, send, recv):
        def far(step):
            factor_copy(k, lax.rem(block + step + 1, blocks), own, every, send, recv).wait_send()

        loop(blocks - 1, far)

        @pl.when(jnp.logical_not(stays[k]))
        def _():
            factor_copy(k, block, own, every, send, recv).wait_send()

    def relay(h):
        source = h * cores + core
        return pltpu.make_async_remote_copy(
            src_ref=q_buf.at[source],
            dst_ref=q_buf.at[source],
            send_sem=relay_send.at[h],
            recv_sem=q_recv.at[source],
            device_id={"layer": 1 - core},
            device_id_type=MESH,
        )

    in_args = (in_own, in_all, in_send, in_recv)
    kept_args = (kept_own, kept_all, kept_send, kept_recv)
    for k in range(slots):
        layer_id = assign_ref[core * slots + k]
        if k == 0:
            load_bin.wait()
        loads_x[k].wait()
        in_proj = lax.dot_general(
            bin_buf[layer_id], x_buf[k].reshape(lanes, width), NT, preferred_element_type=jnp.float32
        )
        in_own[k] = in_proj.astype(jnp.bfloat16)
        send_factor(k, *in_args)
        if k == 0:
            load_bout.wait()
        loads_g[k].wait()
        out_proj = lax.dot_general(
            bout_buf[layer_id], g_buf[k].reshape(lanes, width), NT, preferred_element_type=jnp.float32
        )
        kept_own[k, :rank] = (out_proj * keep).astype(jnp.bfloat16)
        kept_own[k, rank:] = dir_rows
        send_factor(k, *kept_args)

    for h in range(chips // cores):
        relay(h).wait_recv()
        relay(h).start()

    row = lax.broadcasted_iota(jnp.int32, (kinds, lanes), 0)
    lane = lax.broadcasted_iota(jnp.int32, (kinds, lanes), 1)
    own_tokens = lane // tokens == lax.rem(row, examples)
    group = 256 // rank

    def product(step):
        near = lax.rem(block + step // (chips // cores), blocks)
        at = near * (chips // cores) + lax.rem(step, chips // cores)
        pltpu.make_async_copy(in_all.at[at], in_all.at[at], in_recv.at[at]).wait()
        pltpu.make_async_copy(kept_all.at[at], kept_all.at[at], kept_recv.at[at]).wait()
        in_block = in_all[at]
        kept_wide[...] = kept_all[at].astype(jnp.float32)
        dirs = kept_wide[rank : rank + 1] + kept_wide[rank + 1 : rank + 2]
        scale = jnp.where(own_tokens, jnp.where(row < examples, 1.0, dirs), 0.0)
        total = None
        for i in range(group):
            left = jnp.concatenate(
                [
                    (kept_wide[a : a + 1] * scale).astype(jnp.bfloat16)
                    for a in range(i, rank, group)
                ],
                axis=0,
            )
            pieces = [jnp.zeros_like(in_block)] * group
            pieces[i] = in_block
            right = jnp.concatenate(pieces, axis=0)
            term = lax.dot_general(left, right, NT, preferred_element_type=jnp.float32)
            total = term if total is None else total + term
        rounded = total.astype(jnp.bfloat16)
        flat = jnp.concatenate(
            [rounded[a * kinds : (a + 1) * kinds] for a in range(rank // group)], axis=1
        )
        grads[pl.ds(pl.multiple_of(at * kinds, kinds), kinds)] = flat

    count = blocks * (chips // cores)
    loop(count, product)

    for h in range(chips // cores):
        source = h * cores + 1 - core
        pltpu.make_async_copy(q_buf.at[source], q_buf.at[source], q_recv.at[source]).wait()
    scores = lax.dot_general(
        q_buf[...].reshape(chips * q_buf.shape[1], features), grads[...], NT, preferred_element_type=jnp.float32
    )
    for place in range(chips * cores):
        part[place] = scores[place * share : (place + 1) * share]

    here = chip * cores + core

    def sum_copy(other):
        place = lax.rem(here + other, chips * cores)
        return pltpu.make_async_remote_copy(
            src_ref=part.at[place],
            dst_ref=sums.at[here],
            send_sem=sum_send.at[other],
            recv_sem=sum_recv.at[here],
            device_id={"dp": base + place // cores, "layer": lax.rem(place, cores)},
            device_id_type=MESH,
        )

    for other in range(1, chips * cores):
        sum_copy(other).start()
    pltpu.make_async_copy(part.at[here], sums.at[here], sum_recv.at[here]).start()
    for place in range(chips * cores):
        pltpu.make_async_copy(sums.at[place], sums.at[place], sum_recv.at[place]).wait()
    by_core = []
    for c in range(cores):
        total = sums[c]
        for j in range(1, chips):
            total = total + sums[j * cores + c]
        by_core.append(total)
    for kind in range(2):
        result[kind] = jnp.concatenate(
            [
                total[:, at * kinds + kind * examples : at * kinds + (kind + 1) * examples]
                for at in range(count)
                for total in by_core
            ],
            axis=1,
        )
    results = [
        pltpu.make_async_copy(result.at[kind], target, result_sem.at[kind])
        for kind, target in enumerate((scores_hbm, tangent_hbm))
    ]
    for copy in results:
        copy.start()

    for k in range(slots):

        @pl.when(jnp.logical_not(stays[k]))
        def _():
            q_copy(k).wait_send()

        sent_factor(k, *in_args)
        sent_factor(k, *kept_args)
    for h in range(chips // cores):
        relay(h).wait_send()
    for other in range(1, chips * cores):
        sum_copy(other).wait_send()
    for copy in results:
        copy.wait()


def per_device(blocks, x, g, ids, codes, table, assignment, basis_in, basis_out, query):
    examples, slots, tokens, width = x.shape
    chips, rank = basis_in.shape[:2]
    cores = chips // slots
    lanes = examples * tokens
    features = rank * rank
    count = blocks * (chips // cores)
    kinds = 2 * examples
    queries = query.shape[0]
    share = queries // cores
    hbm = pl.BlockSpec(memory_space=pltpu.HBM)
    bf16, f32 = jnp.bfloat16, jnp.float32
    dma = pltpu.SemaphoreType.DMA
    return pl.pallas_call(
        functools.partial(kernel, blocks),
        out_shape=(jax.ShapeDtypeStruct((share, count * cores * examples), f32),) * 2,
        in_specs=[hbm] * 9,
        out_specs=(hbm, hbm),
        scratch_shapes=[
            pltpu.VMEM((slots, examples, tokens, width), bf16),
            pltpu.VMEM((slots, examples, tokens, width), bf16),
            pltpu.VMEM(basis_in.shape, bf16),
            pltpu.VMEM(basis_out.shape, bf16),
            pltpu.VMEM((chips, queries, features), bf16),
            pltpu.VMEM((slots, rank, lanes), bf16),
            pltpu.VMEM((slots, rank + 16, lanes), bf16),
            pltpu.VMEM((count, rank, lanes), bf16),
            pltpu.VMEM((count, rank + 16, lanes), bf16),
            pltpu.VMEM((rank + 16, lanes), f32),
            pltpu.VMEM((count * kinds, features), bf16),
            pltpu.VMEM((chips * cores, share, count * kinds), f32),
            pltpu.VMEM((chips * cores, share, count * kinds), f32),
            pltpu.VMEM(ids.shape, jnp.int32),
            pltpu.VMEM(codes.shape, jnp.int32),
            pltpu.SMEM(table.shape, f32),
            pltpu.SMEM(assignment.shape, jnp.int32),
            pltpu.VMEM((2, share, count * cores * examples), f32),
            dma((slots, 2)),
            dma((2,)),
            dma((slots,)),
            dma((chips,)),
            dma((chips // cores,)),
            dma((slots, blocks)),
            dma((slots, blocks)),
            dma((count,)),
            dma((count,)),
            dma((chips * cores,)),
            dma((chips * cores,)),
            dma((4,)),
            dma((2,)),
        ],
        compiler_params=pltpu.CompilerParams(
            collective_id=0, has_side_effects=True, vmem_limit_bytes=48 * 1024 * 1024
        ),
    )(*[pltpu.with_memory_space_constraint(a, pltpu.HBM) for a in (x, g, ids, codes, table, assignment, basis_in, basis_out, query)])


def solution(mesh):
    placed = (
        P(("grp", "dp"), "layer", None, None),
        P(("grp", "dp"), "layer", None, None),
        P(("grp", "dp"), None),
        P(("grp", "dp"), None),
        P(),
        P(),
        P(),
        P(),
        P(("grp", "dp"), "layer"),
    )

    def run(*args):
        chips = args[5].shape[0]
        return jax.shard_map(
            functools.partial(per_device, mesh.shape["dp"] // chips),
            mesh=mesh,
            in_specs=placed,
            out_specs=(P(("dp", "layer"), "grp"), P(("dp", "layer"), "grp")),
            check_vma=False,
        )(*args)

    return run
```

```python
import functools

import jax
import jax.numpy as jnp
from jax import lax
from jax.experimental import pallas as pl
from jax.experimental.pallas import tpu as pltpu
from jax.sharding import PartitionSpec as P

pad_token = 128001
MESH = pl.DeviceIdType.MESH
NT = (((1,), (1,)), ((), ()))


def loop(count, body):
    if count <= 4:
        for step in range(count):
            body(step)
    else:
        lax.fori_loop(0, count, lambda step, carry: (body(step), carry)[1], 0)


def kernel(
    blocks, x_hbm, g_hbm, ids_hbm, codes_hbm, table_hbm, assign_hbm, bin_hbm, bout_hbm, q_hbm,
    terms,
    x_buf, g_buf, bin_buf, bout_buf, q_buf, in_own, kept_own, in_all, kept_all, kept_wide, grads, part, sums,
    ids_ref, codes_ref, table_ref, assign_ref,
    load_sem, basis_sem, q_send, q_recv, relay_send, in_send, kept_send, in_recv, kept_recv, sum_send, sum_recv, small_sem,
):
    examples, slots, tokens, width = x_hbm.shape
    chips, rank = bin_hbm.shape[:2]
    lanes = examples * tokens
    features = rank * rank
    cores = chips // slots
    kinds = 2 * examples
    share = q_hbm.shape[0] // cores
    grp_dp = lax.axis_index("dp")
    core = lax.axis_index("layer")
    block = grp_dp // chips
    chip = lax.rem(grp_dp, chips)
    base = block * chips

    load_bin = pltpu.make_async_copy(bin_hbm, bin_buf, basis_sem.at[0])
    load_bout = pltpu.make_async_copy(bout_hbm, bout_buf, basis_sem.at[1])
    loads_x = [pltpu.make_async_copy(x_hbm.at[:, k], x_buf.at[k], load_sem.at[k, 0]) for k in range(slots)]
    loads_g = [pltpu.make_async_copy(g_hbm.at[:, k], g_buf.at[k], load_sem.at[k, 1]) for k in range(slots)]
    smalls = [
        pltpu.make_async_copy(source, target, small_sem.at[at])
        for at, (source, target) in enumerate(
            ((assign_hbm, assign_ref), (table_hbm, table_ref), (ids_hbm, ids_ref), (codes_hbm, codes_ref))
        )
    ]
    for small in smalls:
        small.start()
    load_bin.start()
    loads_x[0].start()
    load_bout.start()
    loads_g[0].start()
    for k in range(1, slots):
        loads_x[k].start()
        loads_g[k].start()

    barrier = pltpu.get_barrier_semaphore()
    for other in range(1, chips * cores):
        place = lax.rem(chip * cores + core + other, chips * cores)
        pl.semaphore_signal(
            barrier, inc=1, device_id={"dp": base + place // cores, "layer": lax.rem(place, cores)}, device_id_type=MESH
        )

    def greet(step):
        far = lax.rem(block + step + 1, blocks) * chips
        for k in range(slots):
            pl.semaphore_signal(
                barrier, inc=1, device_id={"dp": far + k * cores + core, "layer": chip // slots}, device_id_type=MESH
            )

    loop(blocks - 1, greet)
    pl.semaphore_wait(barrier, chips * cores - 1 + slots * (blocks - 1))

    to_core = lax.rem(chip, cores)
    slot_of = [core * slots + k for k in range(slots)]
    stays = [jnp.logical_and(chip == slot_of[k], to_core == core) for k in range(slots)]

    def q_copy(k):
        return pltpu.make_async_remote_copy(
            src_ref=q_hbm.at[:, pl.ds(k * features, features)],
            dst_ref=q_buf.at[chip],
            send_sem=q_send.at[k],
            recv_sem=q_recv.at[chip],
            device_id={"dp": base + slot_of[k], "layer": to_core},
            device_id_type=MESH,
        )

    for k in range(slots):

        @pl.when(jnp.logical_not(stays[k]))
        def _():
            q_copy(k).start()

        @pl.when(stays[k])
        def _():
            pltpu.make_async_copy(
                q_hbm.at[:, pl.ds(k * features, features)], q_buf.at[chip], q_recv.at[chip]
            ).start()

    for small in smalls:
        small.wait()
    ids = ids_ref[...]
    codes = codes_ref[...]
    keep8 = (ids != pad_token).astype(jnp.float32)
    dir8 = jnp.zeros(codes.shape, jnp.float32)
    for code in range(table_ref.shape[0]):
        dir8 = jnp.where(codes == code, table_ref[code], dir8)
    keep = jnp.concatenate([keep8[e : e + 1] for e in range(examples)], axis=1)
    direction = jnp.concatenate([dir8[e : e + 1] for e in range(examples)], axis=1)
    dir_high = direction.astype(jnp.bfloat16).astype(jnp.float32)
    dir_low = direction - dir_high
    row16 = lax.broadcasted_iota(jnp.int32, (16, lanes), 0)
    dir_rows = jnp.where(row16 == 0, dir_high, jnp.where(row16 == 1, dir_low, 0.0)).astype(jnp.bfloat16)

    mine = block * slots + chip // cores

    def factor_copy(k, far_block, own, every, send, recv):
        return pltpu.make_async_remote_copy(
            src_ref=own.at[k],
            dst_ref=every.at[mine],
            send_sem=send.at[k, far_block],
            recv_sem=recv.at[mine],
            device_id={"dp": far_block * chips + slot_of[k], "layer": to_core},
            device_id_type=MESH,
        )

    def send_factor(k, own, every, send, recv):
        def far(step):
            factor_copy(k, lax.rem(block + step + 1, blocks), own, every, send, recv).start()

        loop(blocks - 1, far)

        @pl.when(jnp.logical_not(stays[k]))
        def _():
            factor_copy(k, block, own, every, send, recv).start()

        @pl.when(stays[k])
        def _():
            pltpu.make_async_copy(own.at[k], every.at[mine], recv.at[mine]).start()

    def sent_factor(k, own, every, send, recv):
        def far(step):
            factor_copy(k, lax.rem(block + step + 1, blocks), own, every, send, recv).wait_send()

        loop(blocks - 1, far)

        @pl.when(jnp.logical_not(stays[k]))
        def _():
            factor_copy(k, block, own, every, send, recv).wait_send()

    def relay(h):
        source = h * cores + core
        return pltpu.make_async_remote_copy(
            src_ref=q_buf.at[source],
            dst_ref=q_buf.at[source],
            send_sem=relay_send.at[h],
            recv_sem=q_recv.at[source],
            device_id={"layer": 1 - core},
            device_id_type=MESH,
        )

    in_args = (in_own, in_all, in_send, in_recv)
    kept_args = (kept_own, kept_all, kept_send, kept_recv)
    for k in range(slots):
        layer_id = assign_ref[core * slots + k]
        if k == 0:
            load_bin.wait()
        loads_x[k].wait()
        in_proj = lax.dot_general(
            bin_buf[layer_id], x_buf[k].reshape(lanes, width), NT, preferred_element_type=jnp.float32
        )
        in_own[k] = in_proj.astype(jnp.bfloat16)
        send_factor(k, *in_args)
        if k == 0:
            load_bout.wait()
        loads_g[k].wait()
        out_proj = lax.dot_general(
            bout_buf[layer_id], g_buf[k].reshape(lanes, width), NT, preferred_element_type=jnp.float32
        )
        kept_own[k, :rank] = (out_proj * keep).astype(jnp.bfloat16)
        kept_own[k, rank:] = dir_rows
        send_factor(k, *kept_args)

    for h in range(chips // cores):
        relay(h).wait_recv()
        relay(h).start()

    row = lax.broadcasted_iota(jnp.int32, (kinds, lanes), 0)
    lane = lax.broadcasted_iota(jnp.int32, (kinds, lanes), 1)
    own_tokens = lane // tokens == lax.rem(row, examples)
    group = 256 // rank

    def product(step):
        near = lax.rem(block + step // (chips // cores), blocks)
        at = near * (chips // cores) + lax.rem(step, chips // cores)
        pltpu.make_async_copy(in_all.at[at], in_all.at[at], in_recv.at[at]).wait()
        pltpu.make_async_copy(kept_all.at[at], kept_all.at[at], kept_recv.at[at]).wait()
        in_block = in_all[at]
        kept_wide[...] = kept_all[at].astype(jnp.float32)
        dirs = kept_wide[rank : rank + 1] + kept_wide[rank + 1 : rank + 2]
        scale = jnp.where(own_tokens, jnp.where(row < examples, 1.0, dirs), 0.0)
        total = None
        for i in range(group):
            left = jnp.concatenate(
                [
                    (kept_wide[a : a + 1] * scale).astype(jnp.bfloat16)
                    for a in range(i, rank, group)
                ],
                axis=0,
            )
            pieces = [jnp.zeros_like(in_block)] * group
            pieces[i] = in_block
            right = jnp.concatenate(pieces, axis=0)
            term = lax.dot_general(left, right, NT, preferred_element_type=jnp.float32)
            total = term if total is None else total + term
        rounded = total.astype(jnp.bfloat16)
        flat = jnp.concatenate(
            [rounded[a * kinds : (a + 1) * kinds] for a in range(rank // group)], axis=1
        )
        grads[pl.ds(pl.multiple_of(at * kinds, kinds), kinds)] = flat

    count = blocks * (chips // cores)
    loop(count, product)

    for h in range(chips // cores):
        source = h * cores + 1 - core
        pltpu.make_async_copy(q_buf.at[source], q_buf.at[source], q_recv.at[source]).wait()
    scores = lax.dot_general(
        q_buf[...].reshape(chips * q_buf.shape[1], features), grads[...], NT, preferred_element_type=jnp.float32
    )
    for place in range(chips * cores):
        part[place, :, : count * kinds] = scores[place * share : (place + 1) * share]

    here = chip * cores + core

    def sum_copy(other):
        place = lax.rem(here + other, chips * cores)
        return pltpu.make_async_remote_copy(
            src_ref=part.at[place],
            dst_ref=sums.at[here],
            send_sem=sum_send.at[other],
            recv_sem=sum_recv.at[here],
            device_id={"dp": base + place // cores, "layer": lax.rem(place, cores)},
            device_id_type=MESH,
        )

    for other in range(1, chips * cores):
        sum_copy(other).start()
    pltpu.make_async_copy(part.at[here], sums.at[here], sum_recv.at[here]).start()
    for place in range(chips * cores):
        pltpu.make_async_copy(sums.at[place], sums.at[place], sum_recv.at[place]).wait()
    by_core = []
    for c in range(cores):
        total = sums[c]
        for j in range(1, chips):
            total = total + sums[j * cores + c]
        by_core.append(total)
    empty = jnp.zeros((share, examples), jnp.float32)
    for c in range(cores):
        for kind in range(2):
            terms[c, kind] = jnp.concatenate(
                [
                    by_core[c][:, at * kinds + kind * examples : at * kinds + (kind + 1) * examples]
                    if other == c
                    else empty
                    for at in range(count)
                    for other in range(cores)
                ],
                axis=1,
            )

    for k in range(slots):

        @pl.when(jnp.logical_not(stays[k]))
        def _():
            q_copy(k).wait_send()

        sent_factor(k, *in_args)
        sent_factor(k, *kept_args)
    for h in range(chips // cores):
        relay(h).wait_send()
    for other in range(1, chips * cores):
        sum_copy(other).wait_send()


def per_device(blocks, x, g, ids, codes, table, assignment, basis_in, basis_out, query):
    examples, slots, tokens, width = x.shape
    chips, rank = basis_in.shape[:2]
    cores = chips // slots
    lanes = examples * tokens
    features = rank * rank
    count = blocks * (chips // cores)
    kinds = 2 * examples
    queries = query.shape[0]
    share = queries // cores
    hbm = pl.BlockSpec(memory_space=pltpu.HBM)
    bf16, f32 = jnp.bfloat16, jnp.float32
    dma = pltpu.SemaphoreType.DMA
    operands = (x, g, ids, codes, table, assignment, basis_in, basis_out, query)
    terms = pl.pallas_call(
        functools.partial(kernel, blocks),
        out_shape=jax.ShapeDtypeStruct((cores, 2, share, count * cores * examples), f32),
        in_specs=[hbm] * 9,
        out_specs=pl.BlockSpec(memory_space=pltpu.VMEM),
        scratch_shapes=[
            pltpu.VMEM((slots, examples, tokens, width), bf16),
            pltpu.VMEM((slots, examples, tokens, width), bf16),
            pltpu.VMEM(basis_in.shape, bf16),
            pltpu.VMEM(basis_out.shape, bf16),
            pltpu.VMEM((chips, queries, features), bf16),
            pltpu.VMEM((slots, rank, lanes), bf16),
            pltpu.VMEM((slots, rank + 16, lanes), bf16),
            pltpu.VMEM((count, rank, lanes), bf16),
            pltpu.VMEM((count, rank + 16, lanes), bf16),
            pltpu.VMEM((rank + 16, lanes), f32),
            pltpu.VMEM((count * kinds, features), bf16),
            pltpu.VMEM((chips * cores, share, -(-count * kinds // 128) * 128), f32),
            pltpu.VMEM((chips * cores, share, -(-count * kinds // 128) * 128), f32),
            pltpu.VMEM(ids.shape, jnp.int32),
            pltpu.VMEM(codes.shape, jnp.int32),
            pltpu.SMEM(table.shape, f32),
            pltpu.SMEM(assignment.shape, jnp.int32),
            dma((slots, 2)),
            dma((2,)),
            dma((slots,)),
            dma((chips,)),
            dma((chips // cores,)),
            dma((slots, blocks)),
            dma((slots, blocks)),
            dma((count,)),
            dma((count,)),
            dma((chips * cores,)),
            dma((chips * cores,)),
            dma((4,)),
        ],
        compiler_params=pltpu.CompilerParams(
            collective_id=0, has_side_effects=True, vmem_limit_bytes=48 * 1024 * 1024
        ),
    )(*[pltpu.with_memory_space_constraint(operand, pltpu.HBM) for operand in operands])
    both = terms[0]
    for c in range(1, cores):
        both = both + terms[c]
    return both[0], both[1]


def solution(mesh):
    placed = (
        P(("grp", "dp"), "layer", None, None),
        P(("grp", "dp"), "layer", None, None),
        P(("grp", "dp"), None),
        P(("grp", "dp"), None),
        P(),
        P(),
        P(),
        P(),
        P(("grp", "dp"), "layer"),
    )

    def run(*args):
        chips = args[5].shape[0]
        return jax.shard_map(
            functools.partial(per_device, mesh.shape["dp"] // chips),
            mesh=mesh,
            in_specs=placed,
            out_specs=(P(("dp", "layer"), "grp"), P(("dp", "layer"), "grp")),
            check_vma=False,
        )(*args)

    return run
```
